32 devices in a mesh: ctx: 8 (over z, x), head: 4 (over y, core).
Axes of the slice: x: 2, y: 2, z: 4, core: 2. Of those that a mesh axis runs over, the one named last changes fastest.
Arguments:
- queries: bfloat16 [4096, 8192], P('ctx', 'head'), may hold values from -6 to 6
- keys: bfloat16 [4096, 8192], P('ctx', 'head'), may hold values from -6 to 6
- values: bfloat16 [4096, 8192], P('ctx', 'head'), may hold values from -600 to 600
- out_grad: bfloat16 [4096, 6144], P('ctx', 'head'), may hold values from -6 to 6
- out_weight: bfloat16 [6144, 8192], P('ctx', 'head'), may hold values from -0.078125 to 0.078125
- norm_gain: float32 [8192], P('head'), may hold values from 0.1 to 1.9
- slopes: float32 [64], P('head'), may hold values from 0 to 1, as said below
- resp_lengths: int32 [8], replicated, may hold values from 1 to 2048, as said below
Outputs:
- query_grad: bfloat16 [4096, 8192], P('ctx', 'head')
- key_grad: bfloat16 [4096, 8192], P('ctx', 'head')
- value_grad: bfloat16 [4096, 8192], P('ctx', 'head')
The draws below stay inside these ranges and needn't reach their ends.
Inputs may be any that keep to these rules, and one draw needn't show every extreme that they name: `resp_lengths`: responses are packed in order from position 0 and cover 4096 - 256 / 2 positions; the last 128 positions are padding. The last response is the longest, with 2048 positions. `slopes`: positive decay rates.
All inputs are finite; a program needn't handle non-finite values.
Results may differ from the reference program's by a relative error of at most 0.0063.
Values may be sent and summed in bfloat16 or wider, within the bound.
A program may use at most 192 MiB of HBM per device.

```python
import jax
import jax.numpy as jnp
from jax import lax

D = 6144
HEADS = 64
DH = 128
BLK = 256
RESP = 8
SEQ = 4096


def draw_slopes(key, part):
    key_slow, key_fast, key_pick = jax.random.split(key, 3)
    slow_rates = jnp.exp(jax.random.uniform(key_slow, (HEADS,), jnp.float32, jnp.log(0.3 / SEQ), jnp.log(4.0 / SEQ)))
    fast_rates = jnp.exp(jax.random.uniform(key_fast, (HEADS,), jnp.float32, jnp.log(1.0 / 50.0), jnp.log(1.0 / 30.0)))
    chosen = jax.random.bernoulli(key_pick, 0.5, (HEADS,))
    return jnp.where(chosen, slow_rates, fast_rates).astype(jnp.float32)


def draw_values(key, part):
    key_base = jax.random.fold_in(key, 0)
    base = jax.random.truncated_normal(key_base, -6.0, 6.0, (SEQ, HEADS * DH), jnp.float32)
    return base.astype(jnp.bfloat16)


def draw_resp_lengths(key, part):
    front_total = SEQ // 2 - BLK // 2
    cut_points = jnp.sort(jax.random.permutation(jax.random.fold_in(key, 7), front_total - 1)[:RESP - 2] + 1).astype(jnp.int32)
    bounds = jnp.concatenate([jnp.zeros((1,), jnp.int32), cut_points, jnp.full((1,), front_total, jnp.int32)])
    front_lengths = (bounds[1:] - bounds[:-1]).astype(jnp.int32)
    return jnp.concatenate([front_lengths, jnp.full((1,), SEQ // 2, jnp.int32)]).astype(jnp.int32)


def steps_of(stream_key, extent, cuts, low, top_value):
    def one(axis_at, blocks):
        draws = jax.random.uniform(jax.random.fold_in(jax.random.fold_in(stream_key, 6), axis_at), (blocks,), jnp.float32, low / len(cuts), top_value / len(cuts))
        return jnp.repeat(jnp.exp(draws), extent[axis_at] // blocks).reshape((-1,) + (1,) * (len(extent) - axis_at - 1))

    loudness = one(*cuts[0])
    for cut in cuts[1:]:
        loudness = loudness * one(*cut)
    return loudness


def gaussian(stream_key, extent, deviation, most, cuts=(), kind=jnp.bfloat16):
    drawn = jax.random.normal(stream_key, extent, jnp.float32) * deviation
    if len(cuts) > 0:
        drawn = steps_of(stream_key, extent, cuts, -0.22, 0.18) * drawn
    return jnp.clip(drawn, min=-most, max=most).astype(kind)


def setup_inputs(seed: int = 0) -> dict:
    key_list = jax.random.split(jax.random.key(seed), 9)
    return {
        "queries": gaussian(key_list[0], (SEQ, HEADS * DH), 1.0, 6.0, ((0, 8), (1, 4))),
        "keys": gaussian(key_list[1], (SEQ, HEADS * DH), 1.0, 6.0, ((0, 8), (1, 4))),
        "values": draw_values(jax.random.fold_in(key_list[8], 71), 0),
        "out_grad": gaussian(key_list[3], (SEQ, D), 1.0, 6.0, ((0, 8), (1, 4))),
        "out_weight": gaussian(key_list[4], (D, HEADS * DH), D ** -0.5, 0.078125, ((0, 8), (1, 4))),
        "norm_gain": jnp.clip(1.0 + 0.18 * jax.random.normal(key_list[5], (HEADS * DH,), jnp.float32), 0.1, 1.9),
        "slopes": draw_slopes(jax.random.fold_in(key_list[8], 71), 0),
        "resp_lengths": draw_resp_lengths(jax.random.fold_in(key_list[8], 71), 0),
    }


EPSILON = 1e-06

def product(form, left, right):
    left = lax.optimization_barrier(left)
    right = lax.optimization_barrier(right)
    return jnp.einsum(form, left.astype(jnp.float32), right.astype(jnp.float32))

def segment_ids(resp_lengths, positions, responses):
    bounds = jnp.cumsum(resp_lengths).astype(jnp.int32)
    counted = lax.optimization_barrier(jnp.sum((positions[:, None] >= bounds[None, :]).astype(jnp.int32), axis=1)).astype(jnp.int32)
    inside = (counted < responses) & (positions >= 0)
    return jnp.where(inside, counted, -1).astype(jnp.int32)

def block_decays(seg_block, slopes):
    places = jnp.arange(seg_block.shape[0], dtype=jnp.float32)
    distance = places[:, None] - places[None, :]
    allowed = (distance >= 0) & (seg_block[:, None] == seg_block[None, :]) & (seg_block[:, None] >= 0)
    decays = jnp.exp(-slopes[:, None, None] * jnp.maximum(distance, 0.0)[None])
    return jnp.where(allowed[None], decays, 0.0)

def state_update(key_state, prev_seg, key_block, value_block, seg_block, slopes):
    block_len = key_block.shape[0]
    places = jnp.arange(block_len, dtype=jnp.float32)
    final_seg = seg_block[block_len - 1]
    tail_mask = ((seg_block == final_seg) & (final_seg >= 0)).astype(jnp.float32)
    factors = jnp.exp(-slopes[None, :] * (block_len - 1.0 - places)[:, None]) * tail_mask[:, None]
    keys_dec = (key_block.astype(jnp.float32) * factors[:, :, None]).astype(jnp.bfloat16)
    carry_mask = ((final_seg == prev_seg) & (final_seg >= 0)).astype(jnp.float32)
    carry_decay = carry_mask * jnp.exp(-slopes * block_len)
    return carry_decay[:, None, None] * key_state + product('thd,the->hde', keys_dec, value_block)

def back_update(grad_state, next_seg, query_block, grad_block, seg_block, slopes):
    block_len = query_block.shape[0]
    places = jnp.arange(block_len, dtype=jnp.float32)
    lead_seg = seg_block[0]
    lead_mask = ((seg_block == lead_seg) & (lead_seg >= 0)).astype(jnp.float32)
    factors = jnp.exp(-slopes[None, :] * places[:, None]) * lead_mask[:, None]
    queries_dec = (query_block.astype(jnp.float32) * factors[:, :, None]).astype(jnp.bfloat16)
    carry_mask = ((lead_seg == next_seg) & (lead_seg >= 0)).astype(jnp.float32)
    carry_decay = carry_mask * jnp.exp(-slopes * block_len)
    return carry_decay[:, None, None] * grad_state + product('thd,the->hde', queries_dec, grad_block)

def enter_factors(seg_block, prev_seg, slopes):
    places = jnp.arange(seg_block.shape[0], dtype=jnp.float32)
    enter_mask = ((seg_block == prev_seg) & (seg_block >= 0)).astype(jnp.float32)
    return jnp.exp(-slopes[None, :] * (places[:, None] + 1.0)) * enter_mask[:, None]

def exit_factors(seg_block, next_seg, slopes):
    block_len = seg_block.shape[0]
    places = jnp.arange(block_len, dtype=jnp.float32)
    exit_mask = ((seg_block == next_seg) & (seg_block >= 0)).astype(jnp.float32)
    return jnp.exp(-slopes[None, :] * (block_len - places)[:, None]) * exit_mask[:, None]

def forward_block(carried, inputs, slopes):
    key_state, prev_seg = carried
    query_block, key_block, value_block, seg_block = inputs
    decays = block_decays(seg_block, slopes)
    weights = (product('thd,shd->hts', query_block, key_block) * decays).astype(jnp.bfloat16)
    state_used = key_state.astype(jnp.bfloat16)
    inner = product('hts,shd->thd', weights, value_block)
    outer = product('thd,hde->the', query_block, state_used)
    attended = inner + outer * enter_factors(seg_block, prev_seg, slopes)[:, :, None]
    new_state = state_update(key_state, prev_seg, key_block, value_block, seg_block, slopes)
    return ((new_state, seg_block[seg_block.shape[0] - 1]), (attended, state_used))

def backward_block(carried, inputs, slopes):
    grad_state, next_seg = carried
    query_block, key_block, value_block, grad_block, seg_block, prev_seg, state_used = inputs
    decays = block_decays(seg_block, slopes)
    fwd_weights = (product('thd,shd->hts', query_block, key_block) * decays).astype(jnp.bfloat16)
    back_weights = (product('thd,shd->hts', grad_block, value_block) * decays).astype(jnp.bfloat16)
    back_used = grad_state.astype(jnp.bfloat16)
    entering = enter_factors(seg_block, prev_seg, slopes)[:, :, None]
    leaving = exit_factors(seg_block, next_seg, slopes)[:, :, None]
    query_grad = product('hts,shd->thd', back_weights, key_block) + product('the,hde->thd', grad_block, state_used) * entering
    key_grad = product('hts,thd->shd', back_weights, query_block) + product('she,hde->shd', value_block, back_used) * leaving
    value_grad = product('hts,the->she', fwd_weights, grad_block) + product('shd,hde->she', key_block, back_used) * leaving
    new_state = back_update(grad_state, next_seg, query_block, grad_block, seg_block, slopes)
    return ((new_state, seg_block[0]), (query_grad.astype(jnp.bfloat16), key_grad.astype(jnp.bfloat16), value_grad.astype(jnp.bfloat16)))

def reference(queries, keys, values, out_grad, out_weight, norm_gain, slopes, resp_lengths):
    seq_len = queries.shape[0]
    head_count = slopes.shape[0]
    blocks = seq_len // BLK
    block_shape = (blocks, BLK, head_count, DH)
    segments = segment_ids(resp_lengths, jnp.arange(seq_len, dtype=jnp.int32), RESP)
    seg_blocks = segments.reshape(blocks, BLK)
    query_blocks = queries.reshape(block_shape)
    key_blocks = keys.reshape(block_shape)
    value_blocks = values.reshape(block_shape)
    empty = jnp.zeros((head_count, DH, DH), jnp.float32)
    start_seg = jnp.array(-1, jnp.int32)

    def forward_step(carried, inputs):
        return forward_block(carried, inputs, slopes)
    _, (attended, state_used) = lax.scan(forward_step, (empty, start_seg), (query_blocks, key_blocks, value_blocks, seg_blocks))
    attended = attended.reshape(seq_len, head_count * DH)
    rescale = lax.rsqrt(lax.optimization_barrier(jnp.mean(attended * attended, axis=1)) + EPSILON)
    norm_grad = jnp.dot(out_grad, out_weight, preferred_element_type=jnp.float32)
    gained = norm_gain[None, :] * norm_grad
    cross_mean = lax.optimization_barrier(jnp.mean(attended * gained, axis=1))
    out_delta = jnp.where((segments >= 0)[:, None], rescale[:, None] * gained - attended * (rescale ** 3 * cross_mean)[:, None], 0.0).astype(jnp.bfloat16)
    grad_blocks = out_delta.reshape(block_shape)
    prev_segs = jnp.concatenate([start_seg[None], seg_blocks[:-1, BLK - 1]]).astype(jnp.int32)

    def backward_step(carried, inputs):
        return backward_block(carried, inputs, slopes)
    _, (query_grad, key_grad, value_grad) = lax.scan(backward_step, (empty, start_seg), (query_blocks, key_blocks, value_blocks, grad_blocks, seg_blocks, prev_segs, state_used), reverse=True)
    flat = (seq_len, head_count * DH)
    return (query_grad.reshape(flat), key_grad.reshape(flat), value_grad.reshape(flat))
```

```python
import jax
import jax.numpy as jnp
from jax import lax
from jax.experimental import pallas as pl
from jax.experimental.pallas import tpu as pltpu
from jax.sharding import PartitionSpec as P

HEADS = 64
DH = 128
BLK = 256
RESP = 8
EPSILON = 1e-06
VMEM_BYTES = 40 * 1024 * 1024

ENTER, EXIT, TAIL, LEAD, SCALE, CROSS = range(6)


def segment_ids(resp_lengths, positions, responses):
    bounds = jnp.cumsum(resp_lengths)
    counted = jnp.sum((positions[:, None] >= bounds[None, :]).astype(jnp.int32), axis=1)
    inside = (counted < responses) & (positions >= 0)
    return jnp.where(inside, counted, -1)


def dot(left, right, left_dim, right_dim):
    return lax.dot_general(
        left, right, (((left_dim,), (right_dim,)), ((), ())), preferred_element_type=jnp.float32
    )


def places():
    return lax.broadcasted_iota(jnp.int32, (BLK, 1), 0).astype(jnp.float32)


def tile_exp(slope, steps):
    return jnp.exp(jnp.full((1, DH), -slope * steps, jnp.float32))


def decays_of(seg_col, seg_row, slope):
    shape = (BLK, BLK)
    distance = lax.broadcasted_iota(jnp.int32, shape, 0) - lax.broadcasted_iota(jnp.int32, shape, 1)
    allowed = (distance >= 0) & (seg_col == seg_row) & (seg_col >= 0)
    faded = jnp.exp(-slope * jnp.maximum(distance, 0).astype(jnp.float32))
    return jnp.where(allowed, faded, 0.0)


def blocks_of(ref):
    return ref.shape[0] // BLK


def rows(b):
    return pl.ds(b * BLK, BLK)


def weighted(coef_ref, gathered_ref, head):
    total = jnp.zeros((DH, DH), jnp.float32)
    for j in range(gathered_ref.shape[0]):
        total += coef_ref[j, head] * gathered_ref[j, 0].astype(jnp.float32)
    return total


def next_state(state, k, v, table, slope, carry):
    faded = jnp.exp(-slope * (BLK - 1.0 - places())) * table[:, TAIL : TAIL + 1]
    update = dot((k.astype(jnp.float32) * faded).astype(jnp.bfloat16), v, 0, 0)
    if state is None:
        return update
    return (carry * tile_exp(slope, BLK)) * state + update


def summary_kernel(slopes, carries, k_ref, v_ref, table_ref, out_ref):
    slope = slopes[pl.program_id(0)]
    state = None
    for b in range(blocks_of(k_ref)):
        state = next_state(
            state, k_ref[rows(b), :], v_ref[rows(b), :], table_ref[rows(b), :], slope, carries[0, b]
        )
    out_ref[0] = state.astype(out_ref.dtype)


def forward_kernel(
    slopes, carries, coef_ref, gathered_ref, q_ref, k_ref, v_ref, table_ref, col_ref, row_ref,
    attended_ref, used_ref,
):
    head = pl.program_id(0)
    slope = slopes[head]
    state = weighted(coef_ref, gathered_ref, head)
    for b in range(blocks_of(q_ref)):
        q, k, v = q_ref[rows(b), :], k_ref[rows(b), :], v_ref[rows(b), :]
        table = table_ref[rows(b), :]
        decays = decays_of(col_ref[rows(b), :], row_ref[:, rows(b)], slope)
        weights = (dot(q, k, 1, 1) * decays).astype(jnp.bfloat16)
        used = state.astype(jnp.bfloat16)
        used_ref[b, 0] = used
        entering = jnp.exp(-slope * (places() + 1.0)) * table[:, ENTER : ENTER + 1]
        attended_ref[rows(b), :] = dot(weights, v, 1, 0) + entering * dot(q, used, 1, 0)
        state = next_state(state, k, v, table, slope, carries[0, b])


def backward_kernel(
    slopes, carries, q_ref, k_ref, v_ref, gained_ref, attended_ref, used_ref, table_ref, col_ref,
    row_ref, dq_ref, dk_ref, dv_ref, local_ref, total_ref,
):
    slope = slopes[pl.program_id(0)]
    state = jnp.zeros((DH, DH), jnp.float32)
    for b in reversed(range(blocks_of(q_ref))):
        q, k, v = q_ref[rows(b), :], k_ref[rows(b), :], v_ref[rows(b), :]
        table = table_ref[rows(b), :]
        delta = (
            table[:, SCALE : SCALE + 1] * gained_ref[rows(b), :]
            - table[:, CROSS : CROSS + 1] * attended_ref[rows(b), :]
        ).astype(jnp.bfloat16)
        decays = decays_of(col_ref[rows(b), :], row_ref[:, rows(b)], slope)
        fwd_weights = (dot(q, k, 1, 1) * decays).astype(jnp.bfloat16)
        back_weights = (dot(delta, v, 1, 1) * decays).astype(jnp.bfloat16)
        entering = jnp.exp(-slope * (places() + 1.0)) * table[:, ENTER : ENTER + 1]
        dq = dot(back_weights, k, 1, 0) + entering * dot(delta, used_ref[b, 0], 1, 1)
        dq_ref[rows(b), :] = dq.astype(dq_ref.dtype)
        dk_ref[rows(b), :] = dot(back_weights, q, 0, 0)
        dv_ref[rows(b), :] = dot(fwd_weights, delta, 0, 0)
        local_ref[b, 0] = state
        leading = jnp.exp(-slope * places()) * table[:, LEAD : LEAD + 1]
        faded = (q.astype(jnp.float32) * leading).astype(jnp.bfloat16)
        state = (carries[1, b] * tile_exp(slope, BLK)) * state + dot(faded, delta, 0, 0)
    total_ref[0] = state.astype(total_ref.dtype)


def finish_kernel(
    slopes, carries, coef_ref, gathered_ref, k_ref, v_ref, local_ref, table_ref, dk_ref, dv_ref,
    dk_out, dv_out,
):
    head = pl.program_id(0)
    slope = slopes[head]
    entering = weighted(coef_ref, gathered_ref, head)
    count = blocks_of(k_ref)
    for b in range(count):
        reach = carries[2, b] * tile_exp(slope, BLK * (count - 1 - b))
        used = (local_ref[b, 0] + reach * entering).astype(jnp.bfloat16)
        leaving = jnp.exp(-slope * (BLK - places())) * table_ref[rows(b), EXIT : EXIT + 1]
        dk = dk_ref[rows(b), :] + leaving * dot(v_ref[rows(b), :], used, 1, 1)
        dv = dv_ref[rows(b), :] + leaving * dot(k_ref[rows(b), :], used, 1, 0)
        dk_out[rows(b), :] = dk.astype(dk_out.dtype)
        dv_out[rows(b), :] = dv.astype(dv_out.dtype)


def smem():
    return pl.BlockSpec(memory_space=pltpu.SMEM)


def columns(tokens):
    return pl.BlockSpec((tokens, DH), lambda h: (0, h))


def whole(shape):
    return pl.BlockSpec(shape, lambda h: (0,) * len(shape))


def stack(count):
    return pl.BlockSpec((count, 1, DH, DH), lambda h: (0, h, 0, 0))


def one_state():
    return pl.BlockSpec((1, DH, DH), lambda h: (h, 0, 0))


def call(kernel, heads, in_specs, out_specs, out_shape, operands, flops, moved):
    return pl.pallas_call(
        kernel,
        grid=(heads,),
        in_specs=in_specs,
        out_specs=out_specs,
        out_shape=out_shape,
        compiler_params=pltpu.CompilerParams(vmem_limit_bytes=VMEM_BYTES),
        cost_estimate=pl.CostEstimate(flops=flops, bytes_accessed=moved, transcendentals=0),
    )(*operands)


def ring_order(count):
    return [*range(0, count, 2), *range(count - 1 - count % 2, 0, -2)]


def ring_matmul(dy, weight, count):
    order = ring_order(count)
    table = jnp.asarray(order, jnp.int32)
    spot = [order.index(i) for i in range(count)]
    position = jnp.asarray(spot, jnp.int32)[lax.axis_index("ctx")]
    up = [(order[i], order[(i + 1) % count]) for i in range(count)]
    down = [(b, a) for a, b in up]
    depth = weight.shape[0]
    width = dy.shape[2]

    def term(block, step, low):
        owner = table[lax.rem(position + step + count, count)]
        start = owner * depth + low
        part = lax.dynamic_slice(
            dy, (start // width, 0, lax.rem(start, width)), (1, dy.shape[1], block.shape[0])
        )[0]
        return jnp.dot(part, block, preferred_element_type=jnp.float32)

    total = term(weight, 0, 0)
    from_left = from_right = weight
    for step in range(1, (count - 1) // 2 + 1):
        from_left = lax.ppermute(from_left, "ctx", up)
        from_right = lax.ppermute(from_right, "ctx", down)
        total = total + term(from_left, -step, 0)
        total = total + term(from_right, step, 0)
    if count % 2 == 0:
        half = depth // 2
        left = lax.ppermute(from_left[:half], "ctx", up)
        right = lax.ppermute(from_right[half:], "ctx", down)
        total = total + term(left, -(count // 2), 0)
        total = total + term(right, count // 2, half)
    return total


def per_device(queries, keys, values, out_grad, out_weight, norm_gain, slopes, resp_lengths):
    tokens = queries.shape[0]
    heads = slopes.shape[0]
    blocks = tokens // BLK
    width = heads * DH
    count = lax.axis_size("ctx")
    me = lax.axis_index("ctx")
    offset = me * tokens
    positions = offset - 1 + jnp.arange(tokens + 2, dtype=jnp.int32)
    padded = segment_ids(resp_lengths, positions, RESP)
    segments, before, beyond = padded[1:-1], padded[0], padded[-1]
    firsts = segments[::BLK]
    lasts = segments[BLK - 1 :: BLK]
    prevs = jnp.concatenate([before[None], lasts[:-1]])
    nexts = jnp.concatenate([firsts[1:], beyond[None]])

    def spread(per_block):
        return jnp.repeat(per_block, BLK)

    def linked(left, right):
        return ((left == right) & (left >= 0)).astype(jnp.float32)

    masks = [linked(segments, spread(x)) for x in (prevs, nexts, lasts, firsts)]
    valid = (segments >= 0).astype(jnp.float32)
    reach = linked(nexts, jnp.broadcast_to(beyond, nexts.shape)).at[blocks - 1].set(1.0)
    carries = jnp.stack([linked(lasts, prevs), linked(firsts, nexts), reach])
    table = jnp.stack(masks + [valid, valid], axis=1)
    seg_col, seg_row = segments[:, None], segments[None, :]

    spans = jnp.arange(count, dtype=jnp.int32)
    ends = segment_ids(resp_lengths, spans * tokens + (tokens - 1), RESP)
    starts = segment_ids(resp_lengths, spans * tokens, RESP)

    def coefficients(hops, same):
        faded = jnp.exp(-slopes[None, :] * (jnp.maximum(hops, 0) * tokens)[:, None].astype(jnp.float32))
        return jnp.where(((hops >= 0) & same)[:, None], faded, 0.0)

    fwd_coef = coefficients(me - 1 - spans, ends == before)
    bwd_coef = coefficients(spans - me - 1, starts == beyond)

    f32, bf16 = jnp.float32, jnp.bfloat16
    sheet = lambda kind: jax.ShapeDtypeStruct((tokens, width), kind)
    states = jax.ShapeDtypeStruct((heads, DH, DH), bf16)
    per_head = lambda kind: jax.ShapeDtypeStruct((blocks, heads, DH, DH), kind)
    col, table_spec = columns(tokens), whole((tokens, 6))
    seg_specs = [whole((tokens, 1)), whole((1, tokens))]
    unit = 2 * tokens * BLK * width
    size = 2 * tokens * width

    local = call(
        summary_kernel, heads, [smem(), smem(), col, col, table_spec], one_state(), states,
        (slopes, carries, keys, values, table), unit // 2, 2 * size,
    )
    gathered = lax.all_gather(local, "ctx")
    dy = lax.all_gather(out_grad, "head")
    norm_grad = ring_matmul(dy, out_weight, count)

    attended, used = call(
        forward_kernel, heads,
        [smem(), smem(), smem(), stack(count), col, col, col, table_spec, *seg_specs],
        (col, stack(blocks)), (sheet(f32), per_head(bf16)),
        (slopes, carries, fwd_coef, gathered, queries, keys, values, table, seg_col, seg_row),
        3 * unit, 9 * size,
    )
    square_total = lax.psum(jnp.sum(attended * attended, axis=1), "head")
    rescale = lax.rsqrt(square_total / (HEADS * DH) + EPSILON)
    gained = norm_gain[None, :] * norm_grad
    cross_total = lax.psum(jnp.sum(attended * gained, axis=1), "head")
    cross_mean = cross_total / (HEADS * DH)
    back_table = jnp.stack(masks + [valid * rescale, valid * rescale**3 * cross_mean], axis=1)

    dq, dk, dv, inner, total = call(
        backward_kernel, heads,
        [smem(), smem(), col, col, col, col, col, stack(blocks), table_spec, *seg_specs],
        (col, col, col, stack(blocks), one_state()),
        (sheet(bf16), sheet(f32), sheet(f32), per_head(f32), states),
        (slopes, carries, queries, keys, values, gained, attended, used, back_table, seg_col, seg_row),
        6 * unit, 12 * size,
    )
    back_gathered = lax.all_gather(total, "ctx")
    dk, dv = call(
        finish_kernel, heads,
        [smem(), smem(), smem(), stack(count), col, col, stack(blocks), table_spec, col, col],
        (col, col), (sheet(bf16), sheet(bf16)),
        (slopes, carries, bwd_coef, back_gathered, keys, values, inner, table, dk, dv),
        unit, 10 * size,
    )
    return dq, dk, dv


def solution(mesh):
    split = P("ctx", "head")
    return jax.shard_map(
        per_device,
        mesh=mesh,
        in_specs=(split, split, split, split, split, P("head"), P("head"), P()),
        out_specs=(split, split, split),
        check_vma=False,
    )
```

```python
import jax
import jax.numpy as jnp
from jax import lax
from jax.experimental import pallas as pl
from jax.experimental.pallas import tpu as pltpu
from jax.sharding import PartitionSpec as P

HEADS = 64
DH = 128
BLK = 256
RESP = 8
EPSILON = 1e-06
VMEM_BYTES = 40 * 1024 * 1024

ENTER, EXIT, TAIL, LEAD, SCALE, CROSS = range(6)


def segment_ids(resp_lengths, positions, responses):
    bounds = jnp.cumsum(resp_lengths)
    counted = jnp.sum((positions[:, None] >= bounds[None, :]).astype(jnp.int32), axis=1)
    inside = (counted < responses) & (positions >= 0)
    return jnp.where(inside, counted, -1)


def dot(left, right, left_dim, right_dim):
    return lax.dot_general(
        left, right, (((left_dim,), (right_dim,)), ((), ())), preferred_element_type=jnp.float32
    )


def places():
    return lax.broadcasted_iota(jnp.int32, (BLK, 1), 0).astype(jnp.float32)


def tile_exp(slope, steps):
    return jnp.exp(jnp.full((1, DH), -slope * steps, jnp.float32))


def decays_of(seg_col, seg_row, slope):
    shape = (BLK, BLK)
    distance = lax.broadcasted_iota(jnp.int32, shape, 0) - lax.broadcasted_iota(jnp.int32, shape, 1)
    allowed = (distance >= 0) & (seg_col == seg_row) & (seg_col >= 0)
    faded = jnp.exp(-slope * jnp.maximum(distance, 0).astype(jnp.float32))
    return jnp.where(allowed, faded, 0.0)


def blocks_of(ref):
    return ref.shape[0] // BLK


def rows(b):
    return pl.ds(b * BLK, BLK)


def next_state(state, k, v, table, slope, carry):
    faded = jnp.exp(-slope * (BLK - 1.0 - places())) * table[:, TAIL : TAIL + 1]
    update = dot((k.astype(jnp.float32) * faded).astype(jnp.bfloat16), v, 0, 0)
    if state is None:
        return update
    return (carry * tile_exp(slope, BLK)) * state + update


def summary_kernel(slopes, carries, k_ref, v_ref, table_ref, out_ref):
    slope = slopes[pl.program_id(0)]
    state = None
    for b in range(blocks_of(k_ref)):
        state = next_state(
            state, k_ref[rows(b), :], v_ref[rows(b), :], table_ref[rows(b), :], slope, carries[0, b]
        )
    out_ref[0] = state.astype(out_ref.dtype)


def forward_kernel(
    slopes, carries, entering_ref, q_ref, k_ref, v_ref, table_ref, col_ref, row_ref,
    attended_ref, used_ref,
):
    slope = slopes[pl.program_id(0)]
    state = entering_ref[0].astype(jnp.float32)
    for b in range(blocks_of(q_ref)):
        q, k, v = q_ref[rows(b), :], k_ref[rows(b), :], v_ref[rows(b), :]
        table = table_ref[rows(b), :]
        decays = decays_of(col_ref[rows(b), :], row_ref[:, rows(b)], slope)
        weights = (dot(q, k, 1, 1) * decays).astype(jnp.bfloat16)
        used = state.astype(jnp.bfloat16)
        used_ref[b, 0] = used
        entering = jnp.exp(-slope * (places() + 1.0)) * table[:, ENTER : ENTER + 1]
        attended_ref[rows(b), :] = dot(weights, v, 1, 0) + entering * dot(q, used, 1, 0)
        state = next_state(state, k, v, table, slope, carries[0, b])


def delta_kernel(
    slopes, carries, q_ref, gained_ref, attended_ref, table_ref, delta_ref, local_ref, total_ref
):
    slope = slopes[pl.program_id(0)]
    state = jnp.zeros((DH, DH), jnp.float32)
    for b in reversed(range(blocks_of(q_ref))):
        table = table_ref[rows(b), :]
        delta = (
            table[:, SCALE : SCALE + 1] * gained_ref[rows(b), :]
            - table[:, CROSS : CROSS + 1] * attended_ref[rows(b), :]
        ).astype(jnp.bfloat16)
        delta_ref[rows(b), :] = delta
        local_ref[b, 0] = state
        leading = jnp.exp(-slope * places()) * table[:, LEAD : LEAD + 1]
        faded = (q_ref[rows(b), :].astype(jnp.float32) * leading).astype(jnp.bfloat16)
        state = (carries[1, b] * tile_exp(slope, BLK)) * state + dot(faded, delta, 0, 0)
    total_ref[0] = state.astype(total_ref.dtype)


def backward_kernel(
    slopes, q_ref, k_ref, v_ref, delta_ref, used_ref, table_ref, col_ref, row_ref,
    dq_ref, dk_ref, dv_ref,
):
    slope = slopes[pl.program_id(0)]
    for b in range(blocks_of(q_ref)):
        q, k, v = q_ref[rows(b), :], k_ref[rows(b), :], v_ref[rows(b), :]
        delta = delta_ref[rows(b), :]
        decays = decays_of(col_ref[rows(b), :], row_ref[:, rows(b)], slope)
        fwd_weights = (dot(q, k, 1, 1) * decays).astype(jnp.bfloat16)
        back_weights = (dot(delta, v, 1, 1) * decays).astype(jnp.bfloat16)
        entering = jnp.exp(-slope * (places() + 1.0)) * table_ref[rows(b), ENTER : ENTER + 1]
        dq = dot(back_weights, k, 1, 0) + entering * dot(delta, used_ref[b, 0], 1, 1)
        dq_ref[rows(b), :] = dq.astype(dq_ref.dtype)
        dk_ref[rows(b), :] = dot(back_weights, q, 0, 0)
        dv_ref[rows(b), :] = dot(fwd_weights, delta, 0, 0)


def finish_kernel(
    slopes, carries, entering_ref, k_ref, v_ref, local_ref, table_ref, dk_ref, dv_ref,
    dk_out, dv_out,
):
    slope = slopes[pl.program_id(0)]
    entering = entering_ref[0].astype(jnp.float32)
    count = blocks_of(k_ref)
    for b in range(count):
        reach = carries[2, b] * tile_exp(slope, BLK * (count - 1 - b))
        used = (local_ref[b, 0] + reach * entering).astype(jnp.bfloat16)
        leaving = jnp.exp(-slope * (BLK - places())) * table_ref[rows(b), EXIT : EXIT + 1]
        dk = dk_ref[rows(b), :] + leaving * dot(v_ref[rows(b), :], used, 1, 1)
        dv = dv_ref[rows(b), :] + leaving * dot(k_ref[rows(b), :], used, 1, 0)
        dk_out[rows(b), :] = dk.astype(dk_out.dtype)
        dv_out[rows(b), :] = dv.astype(dv_out.dtype)


def smem():
    return pl.BlockSpec(memory_space=pltpu.SMEM)


def columns(tokens):
    return pl.BlockSpec((tokens, DH), lambda h: (0, h))


def whole(shape):
    return pl.BlockSpec(shape, lambda h: (0,) * len(shape))


def stack(count):
    return pl.BlockSpec((count, 1, DH, DH), lambda h: (0, h, 0, 0))


def one_state():
    return pl.BlockSpec((1, DH, DH), lambda h: (h, 0, 0))


def call(kernel, heads, in_specs, out_specs, out_shape, operands, flops, moved):
    return pl.pallas_call(
        kernel,
        grid=(heads,),
        in_specs=in_specs,
        out_specs=out_specs,
        out_shape=out_shape,
        compiler_params=pltpu.CompilerParams(vmem_limit_bytes=VMEM_BYTES),
        cost_estimate=pl.CostEstimate(flops=flops, bytes_accessed=moved, transcendentals=0),
    )(*operands)


def ring_order(count):
    return [*range(0, count, 2), *range(count - 1 - count % 2, 0, -2)]


def ring_matmul(dy, weight, count, beside, forward):
    order = ring_order(count)
    table = jnp.asarray(order, jnp.int32)
    spot = [order.index(i) for i in range(count)]
    position = jnp.asarray(spot, jnp.int32)[lax.axis_index("ctx")]
    up = [(order[i], order[(i + 1) % count]) for i in range(count)]
    down = [(b, a) for a, b in up]
    depth = weight.shape[0]
    width = dy.shape[2]

    def term(block, step, low):
        owner = table[lax.rem(position + step + count, count)]
        start = owner * depth + low
        part = lax.dynamic_slice(
            dy, (start // width, 0, lax.rem(start, width)), (1, dy.shape[1], block.shape[0])
        )[0]
        return jnp.dot(part, block, preferred_element_type=jnp.float32)

    full = (count - 1) // 2
    from_left = lax.ppermute(weight, "ctx", up)
    from_right = lax.ppermute(weight, "ctx", down)
    from_left, from_right, beside = lax.optimization_barrier((from_left, from_right, beside))
    result = forward(*beside)
    total = term(weight, 0, 0)
    for step in range(2, full + 1):
        left = lax.ppermute(from_left, "ctx", up)
        right = lax.ppermute(from_right, "ctx", down)
        total = total + term(from_left, 1 - step, 0)
        total = total + term(from_right, step - 1, 0)
        if step == full:
            result, left, right, total = lax.optimization_barrier((result, left, right, total))
        else:
            left, right, total = lax.optimization_barrier((left, right, total))
        from_left, from_right = left, right
    half = depth // 2
    left = lax.ppermute(from_left[:half], "ctx", up)
    right = lax.ppermute(from_right[half:], "ctx", down)
    total = total + term(from_left, -full, 0)
    total = total + term(from_right, full, 0)
    left, right, total = lax.optimization_barrier((left, right, total))
    total = total + term(left, -(count // 2), 0)
    total = total + term(right, count // 2, half)
    return total, result


def exchange(local, marks, slopes, tokens, reverse):
    count = lax.axis_size("ctx")
    half = local.shape[0] // 2
    index = lambda i: count - 1 - i if reverse else i
    me = index(lax.axis_index("ctx"))
    marks = marks[::-1] if reverse else marks
    high, low = me // 2, me % 2
    swap = [(i, i ^ 1) for i in range(count)]
    f32 = jnp.float32

    def part(array, which):
        return lax.dynamic_slice_in_dim(array, which * half, half)

    def fade(rate, hops, same):
        return jnp.where(same, jnp.exp(-rate * (hops * tokens)), 0.0)[:, None, None]

    mine = part(local, low)
    other = lax.ppermute(part(local, 1 - low), "ctx", swap)
    rate = part(slopes, low)
    first = jnp.where(low == 0, mine, other).astype(f32)
    second = jnp.where(low == 0, other, mine).astype(f32)
    pair = second + fade(rate, 1, marks[2 * high] == marks[2 * high + 1]) * first
    pair = pair.astype(jnp.bfloat16)
    last = marks[jnp.maximum(2 * high - 1, 0)]
    into_first = jnp.zeros(pair.shape, f32)
    for hop in range(1, count // 2):
        moves = [(index(i), index(i + 2 * hop)) for i in range(count - 2 * hop)]
        came = lax.ppermute(pair, "ctx", moves)
        from_high = high - hop
        same = (from_high >= 0) & (marks[jnp.maximum(2 * from_high + 1, 0)] == last)
        into_first = into_first + fade(rate, 2 * (hop - 1), same) * came.astype(f32)
    same = (high > 0) & (marks[2 * high] == last)
    into_second = first + fade(rate, 1, same) * into_first
    into_first, into_second = into_first.astype(jnp.bfloat16), into_second.astype(jnp.bfloat16)
    keep = jnp.where(low == 0, into_first, into_second)
    came = lax.ppermute(jnp.where(low == 0, into_second, into_first), "ctx", swap)
    front = jnp.where(low == 0, keep, came)
    return jnp.concatenate([front, jnp.where(low == 0, came, keep)])


def per_device(queries, keys, values, out_grad, out_weight, norm_gain, slopes, resp_lengths):
    tokens = queries.shape[0]
    heads = slopes.shape[0]
    blocks = tokens // BLK
    width = heads * DH
    count = lax.axis_size("ctx")
    me = lax.axis_index("ctx")
    offset = me * tokens
    positions = offset - 1 + jnp.arange(tokens + 2, dtype=jnp.int32)
    padded = segment_ids(resp_lengths, positions, RESP)
    segments, before, beyond = padded[1:-1], padded[0], padded[-1]
    firsts = segments[::BLK]
    lasts = segments[BLK - 1 :: BLK]
    prevs = jnp.concatenate([before[None], lasts[:-1]])
    nexts = jnp.concatenate([firsts[1:], beyond[None]])

    def spread(per_block):
        return jnp.repeat(per_block, BLK)

    def linked(left, right):
        return ((left == right) & (left >= 0)).astype(jnp.float32)

    masks = [linked(segments, spread(x)) for x in (prevs, nexts, lasts, firsts)]
    valid = (segments >= 0).astype(jnp.float32)
    reach = linked(nexts, jnp.broadcast_to(beyond, nexts.shape)).at[blocks - 1].set(1.0)
    carries = jnp.stack([linked(lasts, prevs), linked(firsts, nexts), reach])
    table = jnp.stack(masks + [valid, valid], axis=1)
    seg_col, seg_row = segments[:, None], segments[None, :]

    spans = jnp.arange(count, dtype=jnp.int32)
    ends = segment_ids(resp_lengths, spans * tokens + (tokens - 1), RESP)
    starts = segment_ids(resp_lengths, spans * tokens, RESP)

    f32, bf16 = jnp.float32, jnp.bfloat16
    sheet = lambda kind: jax.ShapeDtypeStruct((tokens, width), kind)
    states = jax.ShapeDtypeStruct((heads, DH, DH), bf16)
    per_head = lambda kind: jax.ShapeDtypeStruct((blocks, heads, DH, DH), kind)
    col, table_spec = columns(tokens), whole((tokens, 6))
    seg_specs = [whole((tokens, 1)), whole((1, tokens))]
    unit = 2 * tokens * BLK * width
    size = 2 * tokens * width

    def forward(queries, keys, values):
        local = call(
            summary_kernel, heads, [smem(), smem(), col, col, table_spec], one_state(), states,
            (slopes, carries, keys, values, table), unit // 2, 2 * size,
        )
        entering = exchange(local, ends, slopes, tokens, False)
        return call(
            forward_kernel, heads,
            [smem(), smem(), one_state(), col, col, col, table_spec, *seg_specs],
            (col, stack(blocks)), (sheet(f32), per_head(bf16)),
            (slopes, carries, entering, queries, keys, values, table, seg_col, seg_row),
            3 * unit, 6 * size,
        )

    dy = lax.all_gather(out_grad, "head")
    norm_grad, (attended, used) = ring_matmul(
        dy, out_weight, count, (queries, keys, values), forward
    )
    square_total = lax.psum(jnp.sum(attended * attended, axis=1), "head")
    rescale = lax.rsqrt(square_total / (HEADS * DH) + EPSILON)
    gained = norm_gain[None, :] * norm_grad
    cross_total = lax.psum(jnp.sum(attended * gained, axis=1), "head")
    cross_mean = cross_total / (HEADS * DH)
    back_table = jnp.stack(masks + [valid * rescale, valid * rescale**3 * cross_mean], axis=1)

    delta, inner, total = call(
        delta_kernel, heads, [smem(), smem(), col, col, col, table_spec],
        (col, stack(blocks), one_state()), (sheet(bf16), per_head(f32), states),
        (slopes, carries, queries, gained, attended, back_table), unit // 2, 7 * size,
    )
    leaving = exchange(total, starts, slopes, tokens, True)
    dq, dk, dv = call(
        backward_kernel, heads,
        [smem(), col, col, col, col, stack(blocks), table_spec, *seg_specs],
        (col, col, col), (sheet(bf16), sheet(f32), sheet(f32)),
        (slopes, queries, keys, values, delta, used, table, seg_col, seg_row),
        6 * unit, 10 * size,
    )
    dk, dv = call(
        finish_kernel, heads,
        [smem(), smem(), one_state(), col, col, stack(blocks), table_spec, col, col],
        (col, col), (sheet(bf16), sheet(bf16)),
        (slopes, carries, leaving, keys, values, inner, table, dk, dv),
        unit, 10 * size,
    )
    return dq, dk, dv


def solution(mesh):
    split = P("ctx", "head")
    return jax.shard_map(
        per_device,
        mesh=mesh,
        in_specs=(split, split, split, split, split, P("head"), P("head"), P()),
        out_specs=(split, split, split),
        check_vma=False,
    )
```

```python
import jax
import jax.numpy as jnp
from jax import lax
from jax.experimental import pallas as pl
from jax.experimental.pallas import tpu as pltpu
from jax.sharding import PartitionSpec as P

HEADS = 64
DH = 128
BLK = 256
RESP = 8
EPSILON = 1e-06
PER = 2

ENTER, EXIT, TAIL, LEAD, SCALE, CROSS = range(6)


def segment_ids(resp_lengths, positions, responses):
    bounds = jnp.cumsum(resp_lengths)
    counted = jnp.sum((positions[:, None] >= bounds[None, :]).astype(jnp.int32), axis=1)
    inside = (counted < responses) & (positions >= 0)
    return jnp.where(inside, counted, -1)


def dot(left, right, left_dim, right_dim):
    return lax.dot_general(
        left, right, (((left_dim,), (right_dim,)), ((), ())), preferred_element_type=jnp.float32
    )


def places():
    return lax.broadcasted_iota(jnp.int32, (BLK, 1), 0).astype(jnp.float32)


def tile_exp(slope, steps):
    return jnp.exp(jnp.full((1, DH), -slope * steps, jnp.float32))


def decays_of(seg_col, seg_row, slope):
    shape = (BLK, BLK)
    distance = lax.broadcasted_iota(jnp.int32, shape, 0) - lax.broadcasted_iota(jnp.int32, shape, 1)
    allowed = (distance >= 0) & (seg_col == seg_row) & (seg_col >= 0)
    faded = jnp.exp(-slope * jnp.maximum(distance, 0).astype(jnp.float32))
    return jnp.where(allowed, faded, 0.0)


def blocks_of(ref):
    return ref.shape[0] // BLK


def rows(b):
    return pl.ds(b * BLK, BLK)


def next_state(state, k, v, table, slope, carry):
    faded = jnp.exp(-slope * (BLK - 1.0 - places())) * table[:, TAIL : TAIL + 1]
    update = dot((k.astype(jnp.float32) * faded).astype(jnp.bfloat16), v, 0, 0)
    if state is None:
        return update
    return (carry * tile_exp(slope, BLK)) * state + update


def summary_kernel(head, slopes, carries, k_ref, v_ref, table_ref, out_ref):
    slope = slopes[head]
    state = None
    for b in range(blocks_of(k_ref)):
        state = next_state(
            state, k_ref[rows(b), :], v_ref[rows(b), :], table_ref[rows(b), :], slope, carries[0, b]
        )
    out_ref[0] = state.astype(out_ref.dtype)


def forward_kernel(
    head, slopes, carries, entering_ref, q_ref, k_ref, v_ref, table_ref, col_ref, row_ref,
    attended_ref, used_ref,
):
    slope = slopes[head]
    state = entering_ref[0].astype(jnp.float32)
    for b in range(blocks_of(q_ref)):
        q, k, v = q_ref[rows(b), :], k_ref[rows(b), :], v_ref[rows(b), :]
        table = table_ref[rows(b), :]
        decays = decays_of(col_ref[rows(b), :], row_ref[:, rows(b)], slope)
        weights = (dot(q, k, 1, 1) * decays).astype(jnp.bfloat16)
        used = state.astype(jnp.bfloat16)
        used_ref[b, 0] = used
        entering = jnp.exp(-slope * (places() + 1.0)) * table[:, ENTER : ENTER + 1]
        attended_ref[rows(b), :] = dot(weights, v, 1, 0) + entering * dot(q, used, 1, 0)
        state = next_state(state, k, v, table, slope, carries[0, b])


def delta_kernel(
    head, slopes, carries, q_ref, gained_ref, attended_ref, table_ref, delta_ref, local_ref, total_ref
):
    slope = slopes[head]
    state = jnp.zeros((DH, DH), jnp.float32)
    for b in reversed(range(blocks_of(q_ref))):
        table = table_ref[rows(b), :]
        delta = (
            table[:, SCALE : SCALE + 1] * gained_ref[rows(b), :]
            - table[:, CROSS : CROSS + 1] * attended_ref[rows(b), :]
        ).astype(jnp.bfloat16)
        delta_ref[rows(b), :] = delta
        local_ref[b, 0] = state
        leading = jnp.exp(-slope * places()) * table[:, LEAD : LEAD + 1]
        faded = (q_ref[rows(b), :].astype(jnp.float32) * leading).astype(jnp.bfloat16)
        state = (carries[1, b] * tile_exp(slope, BLK)) * state + dot(faded, delta, 0, 0)
    total_ref[0] = state.astype(total_ref.dtype)


def backward_kernel(
    head, slopes, q_ref, k_ref, v_ref, delta_ref, used_ref, table_ref, col_ref, row_ref,
    dq_ref, dk_ref, dv_ref,
):
    slope = slopes[head]
    for b in range(blocks_of(q_ref)):
        q, k, v = q_ref[rows(b), :], k_ref[rows(b), :], v_ref[rows(b), :]
        delta = delta_ref[rows(b), :]
        decays = decays_of(col_ref[rows(b), :], row_ref[:, rows(b)], slope)
        fwd_weights = (dot(q, k, 1, 1) * decays).astype(jnp.bfloat16)
        back_weights = (dot(delta, v, 1, 1) * decays).astype(jnp.bfloat16)
        entering = jnp.exp(-slope * (places() + 1.0)) * table_ref[rows(b), ENTER : ENTER + 1]
        dq = dot(back_weights, k, 1, 0) + entering * dot(delta, used_ref[b, 0], 1, 1)
        dq_ref[rows(b), :] = dq.astype(dq_ref.dtype)
        dk_ref[rows(b), :] = dot(back_weights, q, 0, 0)
        dv_ref[rows(b), :] = dot(fwd_weights, delta, 0, 0)


def finish_kernel(
    head, slopes, carries, entering_ref, k_ref, v_ref, local_ref, table_ref, dk_ref, dv_ref,
    dk_out, dv_out,
):
    slope = slopes[head]
    entering = entering_ref[0].astype(jnp.float32)
    count = blocks_of(k_ref)
    for b in range(count):
        reach = carries[2, b] * tile_exp(slope, BLK * (count - 1 - b))
        used = (local_ref[b, 0] + reach * entering).astype(jnp.bfloat16)
        leaving = jnp.exp(-slope * (BLK - places())) * table_ref[rows(b), EXIT : EXIT + 1]
        dk = dk_ref[rows(b), :] + leaving * dot(v_ref[rows(b), :], used, 1, 1)
        dv = dv_ref[rows(b), :] + leaving * dot(k_ref[rows(b), :], used, 1, 0)
        dk_out[rows(b), :] = dk.astype(dk_out.dtype)
        dv_out[rows(b), :] = dv.astype(dv_out.dtype)


def smem():
    return "smem", pl.BlockSpec(memory_space=pltpu.SMEM)


def columns(tokens):
    return "columns", pl.BlockSpec((tokens, PER * DH), lambda h: (0, h))


def whole(shape):
    return "whole", pl.BlockSpec(shape, lambda h: (0,) * len(shape))


def stack(count):
    return "stack", pl.BlockSpec((count, PER, DH, DH), lambda h: (0, h, 0, 0))


def one_state():
    return "state", pl.BlockSpec((PER, DH, DH), lambda h: (h, 0, 0))


def view(kind, ref, i):
    if kind == "columns":
        return ref.at[:, pl.ds(i * DH, DH)]
    if kind == "stack":
        return ref.at[:, pl.ds(i, 1)]
    if kind == "state":
        return ref.at[pl.ds(i, 1)]
    return ref


def call(kernel, heads, in_specs, out_specs, out_shape, operands, flops, moved):
    kinds = [kind for kind, _ in (*in_specs, *out_specs)]

    def step(*refs):
        for i in range(PER):
            head = pl.program_id(0) * PER + i
            kernel(head, *[view(kind, ref, i) for kind, ref in zip(kinds, refs)])

    return pl.pallas_call(
        step,
        grid=(heads // PER,),
        in_specs=[spec for _, spec in in_specs],
        out_specs=[spec for _, spec in out_specs],
        out_shape=out_shape,
        cost_estimate=pl.CostEstimate(flops=flops, bytes_accessed=moved, transcendentals=0),
    )(*operands)


def ring_order(count):
    return [*range(0, count, 2), *range(count - 1 - count % 2, 0, -2)]


def ring_matmul(dy, weight, count, stages):
    order = ring_order(count)
    table = jnp.asarray(order, jnp.int32)
    spot = [order.index(i) for i in range(count)]
    position = jnp.asarray(spot, jnp.int32)[lax.axis_index("ctx")]
    up = [(order[i], order[(i + 1) % count]) for i in range(count)]
    down = [(b, a) for a, b in up]
    depth = weight.shape[0]
    width = dy.shape[2]

    def term(block, step, low):
        owner = table[lax.rem(position + step + count, count)]
        start = owner * depth + low
        part = lax.dynamic_slice(
            dy, (start // width, 0, lax.rem(start, width)), (1, dy.shape[1], block.shape[0])
        )[0]
        return jnp.dot(part, block, preferred_element_type=jnp.float32)

    full = (count - 1) // 2
    half = depth // 2
    result = next(stages)
    left = lax.ppermute(weight, "ctx", up)
    right = lax.ppermute(weight, "ctx", down)
    left, right, result = lax.optimization_barrier((left, right, result))
    total = term(weight, 0, 0)
    for step in range(1, full + 1):
        last = step == full
        result = stages.send(result)
        new_left = lax.ppermute(left[:half] if last else left, "ctx", up)
        new_right = lax.ppermute(right[half:] if last else right, "ctx", down)
        total = total + term(left, -step, 0)
        total = total + term(right, step, 0)
        left, right, total, result = lax.optimization_barrier(
            (new_left, new_right, total, result)
        )
    total = total + term(left, -(count // 2), 0)
    total = total + term(right, count // 2, half)
    return total, result


def exchange(local, marks, slopes, tokens, reverse):
    count = lax.axis_size("ctx")
    half = local.shape[0] // 2
    index = lambda i: count - 1 - i if reverse else i
    me = index(lax.axis_index("ctx"))
    marks = marks[::-1] if reverse else marks
    high, low = me // 2, me % 2
    swap = [(i, i ^ 1) for i in range(count)]
    f32 = jnp.float32

    def part(array, which):
        return lax.dynamic_slice_in_dim(array, which * half, half)

    def fade(rate, hops, same):
        return jnp.where(same, jnp.exp(-rate * (hops * tokens)), 0.0)[:, None, None]

    mine = part(local, low)
    other = yield lax.ppermute(part(local, 1 - low), "ctx", swap)
    rate = part(slopes, low)
    first = jnp.where(low == 0, mine, other).astype(f32)
    second = jnp.where(low == 0, other, mine).astype(f32)
    pair = second + fade(rate, 1, marks[2 * high] == marks[2 * high + 1]) * first
    pair = pair.astype(jnp.bfloat16)
    last = marks[jnp.maximum(2 * high - 1, 0)]
    into_first = jnp.zeros(pair.shape, f32)
    hops = range(1, count // 2)
    moves = [[(index(i), index(i + 2 * hop)) for i in range(count - 2 * hop)] for hop in hops]
    arrived = yield [lax.ppermute(pair, "ctx", move) for move in moves]
    for hop, came in zip(hops, arrived):
        from_high = high - hop
        same = (from_high >= 0) & (marks[jnp.maximum(2 * from_high + 1, 0)] == last)
        into_first = into_first + fade(rate, 2 * (hop - 1), same) * came.astype(f32)
    same = (high > 0) & (marks[2 * high] == last)
    into_second = first + fade(rate, 1, same) * into_first
    into_first, into_second = into_first.astype(jnp.bfloat16), into_second.astype(jnp.bfloat16)
    keep = jnp.where(low == 0, into_first, into_second)
    came = yield lax.ppermute(jnp.where(low == 0, into_second, into_first), "ctx", swap)
    front = jnp.where(low == 0, keep, came)
    return jnp.concatenate([front, jnp.where(low == 0, came, keep)])


def finish_exchange(steps, arrived):
    try:
        steps.send(arrived)
    except StopIteration as end:
        return end.value


def per_device(queries, keys, values, out_grad, out_weight, norm_gain, slopes, resp_lengths):
    tokens = queries.shape[0]
    heads = slopes.shape[0]
    blocks = tokens // BLK
    width = heads * DH
    count = lax.axis_size("ctx")
    me = lax.axis_index("ctx")
    offset = me * tokens
    positions = offset - 1 + jnp.arange(tokens + 2, dtype=jnp.int32)
    padded = segment_ids(resp_lengths, positions, RESP)
    segments, before, beyond = padded[1:-1], padded[0], padded[-1]
    firsts = segments[::BLK]
    lasts = segments[BLK - 1 :: BLK]
    prevs = jnp.concatenate([before[None], lasts[:-1]])
    nexts = jnp.concatenate([firsts[1:], beyond[None]])

    def spread(per_block):
        return jnp.repeat(per_block, BLK)

    def linked(left, right):
        return ((left == right) & (left >= 0)).astype(jnp.float32)

    masks = [linked(segments, spread(x)) for x in (prevs, nexts, lasts, firsts)]
    valid = (segments >= 0).astype(jnp.float32)
    reach = linked(nexts, jnp.broadcast_to(beyond, nexts.shape)).at[blocks - 1].set(1.0)
    carries = jnp.stack([linked(lasts, prevs), linked(firsts, nexts), reach])
    table = jnp.stack(masks + [valid, valid], axis=1)
    seg_col, seg_row = segments[:, None], segments[None, :]

    spans = jnp.arange(count, dtype=jnp.int32)
    ends = segment_ids(resp_lengths, spans * tokens + (tokens - 1), RESP)
    starts = segment_ids(resp_lengths, spans * tokens, RESP)

    f32, bf16 = jnp.float32, jnp.bfloat16
    sheet = lambda kind: jax.ShapeDtypeStruct((tokens, width), kind)
    states = jax.ShapeDtypeStruct((heads, DH, DH), bf16)
    per_head = lambda kind: jax.ShapeDtypeStruct((blocks, heads, DH, DH), kind)
    col, table_spec = columns(tokens), whole((tokens, 6))
    seg_specs = [whole((tokens, 1)), whole((1, tokens))]
    unit = 2 * tokens * BLK * width
    size = 2 * tokens * width

    def forward():
        (local,) = call(
            summary_kernel, heads, [smem(), smem(), col, col, table_spec], [one_state()], [states],
            (slopes, carries, keys, values, table), unit // 2, 2 * size,
        )
        entering = yield from exchange(local, ends, slopes, tokens, False)
        result = call(
            forward_kernel, heads,
            [smem(), smem(), one_state(), col, col, col, table_spec, *seg_specs],
            [col, stack(blocks)], [sheet(f32), per_head(bf16)],
            (slopes, carries, entering, queries, keys, values, table, seg_col, seg_row),
            3 * unit, 6 * size,
        )
        while True:
            result = yield result

    dy = lax.all_gather(out_grad, "head")
    norm_grad, (attended, used) = ring_matmul(dy, out_weight, count, forward())
    square_total = lax.psum(jnp.sum(attended * attended, axis=1), "head")
    rescale = lax.rsqrt(square_total / (HEADS * DH) + EPSILON)
    gained = norm_gain[None, :] * norm_grad
    cross_total = lax.psum(jnp.sum(attended * gained, axis=1), "head")
    cross_mean = cross_total / (HEADS * DH)
    back_table = jnp.stack(masks + [valid * rescale, valid * rescale**3 * cross_mean], axis=1)

    delta, inner, total = call(
        delta_kernel, heads, [smem(), smem(), col, col, col, table_spec],
        [col, stack(blocks), one_state()], [sheet(bf16), per_head(f32), states],
        (slopes, carries, queries, gained, attended, back_table), unit // 2, 7 * size,
    )
    steps = exchange(total, starts, slopes, tokens, True)
    arrived = steps.send(next(steps))
    dq, dk, dv = call(
        backward_kernel, heads,
        [smem(), col, col, col, col, stack(blocks), table_spec, *seg_specs],
        [col, col, col], [sheet(bf16), sheet(f32), sheet(f32)],
        (slopes, queries, keys, values, delta, used, table, seg_col, seg_row),
        6 * unit, 10 * size,
    )
    arrived, dq, dk, dv = lax.optimization_barrier((arrived, dq, dk, dv))
    leaving = finish_exchange(steps, steps.send(arrived))
    dk, dv = call(
        finish_kernel, heads,
        [smem(), smem(), one_state(), col, col, stack(blocks), table_spec, col, col],
        [col, col], [sheet(bf16), sheet(bf16)],
        (slopes, carries, leaving, keys, values, inner, table, dk, dv),
        unit, 10 * size,
    )
    return dq, dk, dv


def solution(mesh):
    split = P("ctx", "head")
    return jax.shard_map(
        per_device,
        mesh=mesh,
        in_specs=(split, split, split, split, split, P("head"), P("head"), P()),
        out_specs=(split, split, split),
        check_vma=False,
    )
```

```python
import jax
import jax.numpy as jnp
from jax import lax
from jax.experimental import pallas as pl
from jax.experimental.pallas import tpu as pltpu
from jax.sharding import PartitionSpec as P

HEADS = 64
DH = 128
BLK = 256
RESP = 8
EPSILON = 1e-06
PER = 2

ENTER, EXIT, TAIL, LEAD, SCALE, CROSS = range(6)


def segment_ids(resp_lengths, positions, responses):
    bounds = jnp.cumsum(resp_lengths)
    counted = jnp.sum((positions[:, None] >= bounds[None, :]).astype(jnp.int32), axis=1)
    inside = (counted < responses) & (positions >= 0)
    return jnp.where(inside, counted, -1)


def dot(left, right, left_dim, right_dim):
    return lax.dot_general(
        left, right, (((left_dim,), (right_dim,)), ((), ())), preferred_element_type=jnp.float32
    )


def places():
    return lax.broadcasted_iota(jnp.int32, (BLK, 1), 0).astype(jnp.float32)


def tile_exp(slope, steps):
    return jnp.exp(jnp.full((1, DH), -slope * steps, jnp.float32))


def decays_of(seg_col, seg_row, slope):
    shape = (BLK, BLK)
    distance = lax.broadcasted_iota(jnp.int32, shape, 0) - lax.broadcasted_iota(jnp.int32, shape, 1)
    allowed = (distance >= 0) & (seg_col == seg_row) & (seg_col >= 0)
    faded = jnp.exp(-slope * jnp.maximum(distance, 0).astype(jnp.float32))
    return jnp.where(allowed, faded, 0.0)


def blocks_of(ref):
    return ref.shape[0] // BLK


def rows(b):
    return pl.ds(b * BLK, BLK)


def next_state(state, k, v, table, slope, carry):
    faded = jnp.exp(-slope * (BLK - 1.0 - places())) * table[:, TAIL : TAIL + 1]
    update = dot((k.astype(jnp.float32) * faded).astype(jnp.bfloat16), v, 0, 0)
    if state is None:
        return update
    return (carry * tile_exp(slope, BLK)) * state + update


def summary_kernel(head, slopes, carries, k_ref, v_ref, table_ref, out_ref):
    slope = slopes[head]
    state = None
    for b in range(blocks_of(k_ref)):
        state = next_state(
            state, k_ref[rows(b), :], v_ref[rows(b), :], table_ref[rows(b), :], slope, carries[0, b]
        )
    out_ref[0] = state.astype(out_ref.dtype)


def forward_kernel(
    head, slopes, carries, entering_ref, q_ref, k_ref, v_ref, table_ref, col_ref, row_ref,
    attended_ref, used_ref,
):
    slope = slopes[head]
    state = entering_ref[0].astype(jnp.float32)
    for b in range(blocks_of(q_ref)):
        q, k, v = q_ref[rows(b), :], k_ref[rows(b), :], v_ref[rows(b), :]
        table = table_ref[rows(b), :]
        decays = decays_of(col_ref[rows(b), :], row_ref[:, rows(b)], slope)
        weights = (dot(q, k, 1, 1) * decays).astype(jnp.bfloat16)
        used = state.astype(jnp.bfloat16)
        used_ref[b, 0] = used
        entering = jnp.exp(-slope * (places() + 1.0)) * table[:, ENTER : ENTER + 1]
        attended_ref[rows(b), :] = dot(weights, v, 1, 0) + entering * dot(q, used, 1, 0)
        state = next_state(state, k, v, table, slope, carries[0, b])


def delta_kernel(
    head, slopes, carries, q_ref, gained_ref, attended_ref, table_ref, delta_ref, local_ref, total_ref
):
    slope = slopes[head]
    state = jnp.zeros((DH, DH), jnp.float32)
    for b in reversed(range(blocks_of(q_ref))):
        table = table_ref[rows(b), :]
        delta = (
            table[:, SCALE : SCALE + 1] * gained_ref[rows(b), :]
            - table[:, CROSS : CROSS + 1] * attended_ref[rows(b), :]
        ).astype(jnp.bfloat16)
        delta_ref[rows(b), :] = delta
        local_ref[b, 0] = state
        leading = jnp.exp(-slope * places()) * table[:, LEAD : LEAD + 1]
        faded = (q_ref[rows(b), :].astype(jnp.float32) * leading).astype(jnp.bfloat16)
        state = (carries[1, b] * tile_exp(slope, BLK)) * state + dot(faded, delta, 0, 0)
    total_ref[0] = state.astype(total_ref.dtype)


def backward_kernel(
    head, slopes, q_ref, k_ref, v_ref, delta_ref, used_ref, table_ref, col_ref, row_ref,
    dq_ref, dk_ref, dv_ref,
):
    slope = slopes[head]
    for b in range(blocks_of(q_ref)):
        q, k, v = q_ref[rows(b), :], k_ref[rows(b), :], v_ref[rows(b), :]
        delta = delta_ref[rows(b), :]
        decays = decays_of(col_ref[rows(b), :], row_ref[:, rows(b)], slope)
        fwd_weights = (dot(q, k, 1, 1) * decays).astype(jnp.bfloat16)
        back_weights = (dot(delta, v, 1, 1) * decays).astype(jnp.bfloat16)
        entering = jnp.exp(-slope * (places() + 1.0)) * table_ref[rows(b), ENTER : ENTER + 1]
        dq = dot(back_weights, k, 1, 0) + entering * dot(delta, used_ref[b, 0], 1, 1)
        dq_ref[rows(b), :] = dq.astype(dq_ref.dtype)
        dk_ref[rows(b), :] = dot(back_weights, q, 0, 0)
        dv_ref[rows(b), :] = dot(fwd_weights, delta, 0, 0)


def finish_kernel(
    head, slopes, carries, entering_ref, k_ref, v_ref, local_ref, table_ref, dk_ref, dv_ref,
    dk_out, dv_out,
):
    slope = slopes[head]
    entering = entering_ref[0].astype(jnp.float32)
    count = blocks_of(k_ref)
    for b in range(count):
        reach = carries[2, b] * tile_exp(slope, BLK * (count - 1 - b))
        used = (local_ref[b, 0] + reach * entering).astype(jnp.bfloat16)
        leaving = jnp.exp(-slope * (BLK - places())) * table_ref[rows(b), EXIT : EXIT + 1]
        dk = dk_ref[rows(b), :] + leaving * dot(v_ref[rows(b), :], used, 1, 1)
        dv = dv_ref[rows(b), :] + leaving * dot(k_ref[rows(b), :], used, 1, 0)
        dk_out[rows(b), :] = dk.astype(dk_out.dtype)
        dv_out[rows(b), :] = dv.astype(dv_out.dtype)


def smem():
    return "smem", pl.BlockSpec(memory_space=pltpu.SMEM)


def columns(tokens):
    return "columns", pl.BlockSpec((tokens, PER * DH), lambda h: (0, h))


def whole(shape):
    return "whole", pl.BlockSpec(shape, lambda h: (0,) * len(shape))


def stack(count):
    return "stack", pl.BlockSpec((count, PER, DH, DH), lambda h: (0, h, 0, 0))


def one_state():
    return "state", pl.BlockSpec((PER, DH, DH), lambda h: (h, 0, 0))


def view(kind, ref, i):
    if kind == "columns":
        return ref.at[:, pl.ds(i * DH, DH)]
    if kind == "stack":
        return ref.at[:, pl.ds(i, 1)]
    if kind == "state":
        return ref.at[pl.ds(i, 1)]
    return ref


def call(kernel, heads, in_specs, out_specs, out_shape, operands, flops, moved):
    kinds = [kind for kind, _ in (*in_specs, *out_specs)]

    def step(*refs):
        for i in range(PER):
            head = pl.program_id(0) * PER + i
            kernel(head, *[view(kind, ref, i) for kind, ref in zip(kinds, refs)])

    return pl.pallas_call(
        step,
        grid=(heads // PER,),
        in_specs=[spec for _, spec in in_specs],
        out_specs=[spec for _, spec in out_specs],
        out_shape=out_shape,
        cost_estimate=pl.CostEstimate(flops=flops, bytes_accessed=moved, transcendentals=0),
    )(*operands)


def ring_order(count):
    return [*range(0, count, 2), *range(count - 1 - count % 2, 0, -2)]


def ring_matmul(dy, weight, count, stages):
    order = ring_order(count)
    table = jnp.asarray(order, jnp.int32)
    spot = [order.index(i) for i in range(count)]
    position = jnp.asarray(spot, jnp.int32)[lax.axis_index("ctx")]
    up = [(order[i], order[(i + 1) % count]) for i in range(count)]
    down = [(b, a) for a, b in up]
    depth = weight.shape[0]
    width = dy.shape[2]

    def term(block, step, low):
        owner = table[lax.rem(position + step + count, count)]
        start = owner * depth + low
        part = lax.dynamic_slice(
            dy, (start // width, 0, lax.rem(start, width)), (1, dy.shape[1], block.shape[0])
        )[0]
        return jnp.dot(part, block, preferred_element_type=jnp.float32)

    full = (count - 1) // 2
    half = depth // 2
    result = next(stages)
    left = lax.ppermute(weight, "ctx", up)
    right = lax.ppermute(weight, "ctx", down)
    left, right, result = lax.optimization_barrier((left, right, result))
    total = term(weight, 0, 0)
    for step in range(1, full + 1):
        last = step == full
        result = stages.send(result)
        new_left = lax.ppermute(left[:half] if last else left, "ctx", up)
        new_right = lax.ppermute(right[half:] if last else right, "ctx", down)
        total = total + term(left, -step, 0)
        total = total + term(right, step, 0)
        if last:
            left, right, total, result = lax.optimization_barrier(
                (new_left, new_right, total, result)
            )
        else:
            left, right = new_left, new_right
            total, result = lax.optimization_barrier((total, result))
    total = total + term(left, -(count // 2), 0)
    total = total + term(right, count // 2, half)
    return total, result


def exchange(local, marks, slopes, tokens, reverse):
    count = lax.axis_size("ctx")
    half = local.shape[0] // 2
    index = lambda i: count - 1 - i if reverse else i
    me = index(lax.axis_index("ctx"))
    marks = marks[::-1] if reverse else marks
    high, low = me // 2, me % 2
    swap = [(i, i ^ 1) for i in range(count)]
    f32 = jnp.float32

    def part(array, which):
        return lax.dynamic_slice_in_dim(array, which * half, half)

    def fade(rate, hops, same):
        return jnp.where(same, jnp.exp(-rate * (hops * tokens)), 0.0)[:, None, None]

    mine = part(local, low)
    other = yield lax.ppermute(part(local, 1 - low), "ctx", swap)
    rate = part(slopes, low)
    first = jnp.where(low == 0, mine, other).astype(f32)
    second = jnp.where(low == 0, other, mine).astype(f32)
    pair = second + fade(rate, 1, marks[2 * high] == marks[2 * high + 1]) * first
    pair = pair.astype(jnp.bfloat16)
    last = marks[jnp.maximum(2 * high - 1, 0)]
    into_first = jnp.zeros(pair.shape, f32)

    def along(state, hop):
        moves = [(index(i), index(i + 2 * hop)) for i in range(count - 2 * hop)]
        return lax.ppermute(state, "ctx", moves)

    def reached(hop, mark):
        from_high = high - hop
        return (from_high >= 0) & (marks[jnp.maximum(2 * from_high + 1, 0)] == mark)

    if reverse:
        hop = 1
        while hop < count // 2:
            came = yield along(pair, hop)
            came = came.astype(f32)
            into_first += fade(rate, 2 * (hop - 1), reached(hop, last)) * came
            covered = fade(rate, 2 * hop, reached(hop, marks[2 * high + 1])) * came
            pair = (pair.astype(f32) + covered).astype(jnp.bfloat16)
            hop *= 2
    else:
        hops = range(1, count // 2)
        arrived = yield [along(pair, hop) for hop in hops]
        for hop, came in zip(hops, arrived):
            into_first += fade(rate, 2 * (hop - 1), reached(hop, last)) * came.astype(f32)
    same = (high > 0) & (marks[2 * high] == last)
    into_second = first + fade(rate, 1, same) * into_first
    into_first, into_second = into_first.astype(jnp.bfloat16), into_second.astype(jnp.bfloat16)
    keep = jnp.where(low == 0, into_first, into_second)
    came = yield lax.ppermute(jnp.where(low == 0, into_second, into_first), "ctx", swap)
    front = jnp.where(low == 0, keep, came)
    return jnp.concatenate([front, jnp.where(low == 0, came, keep)])


def finish_exchange(steps, arrived):
    try:
        while True:
            arrived = steps.send(arrived)
    except StopIteration as end:
        return end.value


def per_device(queries, keys, values, out_grad, out_weight, norm_gain, slopes, resp_lengths):
    tokens = queries.shape[0]
    heads = slopes.shape[0]
    blocks = tokens // BLK
    width = heads * DH
    count = lax.axis_size("ctx")
    me = lax.axis_index("ctx")
    offset = me * tokens
    positions = offset - 1 + jnp.arange(tokens + 2, dtype=jnp.int32)
    padded = segment_ids(resp_lengths, positions, RESP)
    segments, before, beyond = padded[1:-1], padded[0], padded[-1]
    firsts = segments[::BLK]
    lasts = segments[BLK - 1 :: BLK]
    prevs = jnp.concatenate([before[None], lasts[:-1]])
    nexts = jnp.concatenate([firsts[1:], beyond[None]])

    def spread(per_block):
        return jnp.repeat(per_block, BLK)

    def linked(left, right):
        return ((left == right) & (left >= 0)).astype(jnp.float32)

    masks = [linked(segments, spread(x)) for x in (prevs, nexts, lasts, firsts)]
    valid = (segments >= 0).astype(jnp.float32)
    reach = linked(nexts, jnp.broadcast_to(beyond, nexts.shape)).at[blocks - 1].set(1.0)
    carries = jnp.stack([linked(lasts, prevs), linked(firsts, nexts), reach])
    table = jnp.stack(masks + [valid, valid], axis=1)
    seg_col, seg_row = segments[:, None], segments[None, :]

    spans = jnp.arange(count, dtype=jnp.int32)
    ends = segment_ids(resp_lengths, spans * tokens + (tokens - 1), RESP)
    starts = segment_ids(resp_lengths, spans * tokens, RESP)

    f32, bf16 = jnp.float32, jnp.bfloat16
    sheet = lambda kind: jax.ShapeDtypeStruct((tokens, width), kind)
    states = jax.ShapeDtypeStruct((heads, DH, DH), bf16)
    per_head = lambda kind: jax.ShapeDtypeStruct((blocks, heads, DH, DH), kind)
    col, table_spec = columns(tokens), whole((tokens, 6))
    seg_specs = [whole((tokens, 1)), whole((1, tokens))]
    unit = 2 * tokens * BLK * width
    size = 2 * tokens * width

    def forward():
        (local,) = call(
            summary_kernel, heads, [smem(), smem(), col, col, table_spec], [one_state()], [states],
            (slopes, carries, keys, values, table), unit // 2, 2 * size,
        )
        entering = yield from exchange(local, ends, slopes, tokens, False)
        result = call(
            forward_kernel, heads,
            [smem(), smem(), one_state(), col, col, col, table_spec, *seg_specs],
            [col, stack(blocks)], [sheet(f32), per_head(bf16)],
            (slopes, carries, entering, queries, keys, values, table, seg_col, seg_row),
            3 * unit, 6 * size,
        )
        while True:
            result = yield result

    dy = lax.all_gather(out_grad, "head")
    norm_grad, (attended, used) = ring_matmul(dy, out_weight, count, forward())
    square_total = lax.psum(jnp.sum(attended * attended, axis=1), "head")
    rescale = lax.rsqrt(square_total / (HEADS * DH) + EPSILON)
    gained = norm_gain[None, :] * norm_grad
    cross_total = lax.psum(jnp.sum(attended * gained, axis=1), "head")
    cross_mean = cross_total / (HEADS * DH)
    back_table = jnp.stack(masks + [valid * rescale, valid * rescale**3 * cross_mean], axis=1)

    delta, inner, total = call(
        delta_kernel, heads, [smem(), smem(), col, col, col, table_spec],
        [col, stack(blocks), one_state()], [sheet(bf16), per_head(f32), states],
        (slopes, carries, queries, gained, attended, back_table), unit // 2, 7 * size,
    )
    steps = exchange(total, starts, slopes, tokens, True)
    arrived = steps.send(next(steps))
    arrived = steps.send(arrived)
    dq, dk, dv = call(
        backward_kernel, heads,
        [smem(), col, col, col, col, stack(blocks), table_spec, *seg_specs],
        [col, col, col], [sheet(bf16), sheet(f32), sheet(f32)],
        (slopes, queries, keys, values, delta, used, table, seg_col, seg_row),
        6 * unit, 10 * size,
    )
    arrived, dq, dk, dv = lax.optimization_barrier((arrived, dq, dk, dv))
    leaving = finish_exchange(steps, arrived)
    dk, dv = call(
        finish_kernel, heads,
        [smem(), smem(), one_state(), col, col, stack(blocks), table_spec, col, col],
        [col, col], [sheet(bf16), sheet(bf16)],
        (slopes, carries, leaving, keys, values, inner, table, dk, dv),
        unit, 10 * size,
    )
    return dq, dk, dv


def solution(mesh):
    split = P("ctx", "head")
    return jax.shard_map(
        per_device,
        mesh=mesh,
        in_specs=(split, split, split, split, split, P("head"), P("head"), P()),
        out_specs=(split, split, split),
        check_vma=False,
    )
```
